32 devices in a mesh: grp: 2 (over x), own: 16 (over z, y, core).
Axes of the slice: x: 2, y: 2, z: 4, core: 2. Of those that a mesh axis runs over, the one named last changes fastest.
Arguments:
- amps: bfloat16 [896, 128, 128], P(('grp', 'own')), may hold values from -0.35 to 0.35, as said below
- ints: bfloat16 [896, 128, 128], P(('grp', 'own')), may hold values from -0.5 to 0.5, as said below
- pno_energy: float32 [896, 128], P(('grp', 'own')), may hold values from 0.2 to 2, as said below
- occ_energy: float32 [1000], replicated, may hold values from -1 to -0.2
- pair_occ: int32 [2, 896], P(None, ('grp', 'own')), may hold values from 0 to 999, as said below
- mirror: int32 [896], P(('grp', 'own')), may hold values from 0 to 895, as said below
- edge_src: int32 [1536], P(('grp', 'own')), may hold values from 0 to 895, as said below
- edge_dst: int32 [1536], P('grp'), may hold values from 0 to 895, as said below
- edge_fock: float32 [1536], P(('grp', 'own')), may hold values from -6 to 6
- margin: bfloat16 [1536, 128, 128], P(('grp', 'own')), may hold values from -0.15 to 1.15
Outputs:
- residual: bfloat16 [896, 128, 128], P(('grp', 'own'))
The draws below stay inside these ranges and needn't reach their ends.
Inputs may be any that keep to these rules, and one draw needn't show every extreme that they name: `pair_occ`: each pair's two indices differ. The pair at mirror[p] has its two indices swapped. mirror is an involution without fixed points; a pair and its mirror lie in the same grp block of pairs but never on the same device; amps and ints of mirror[p] are the transposes of those of p, and pno_energy is equal. Of one device's pairs at most 2 have their mirror on any one other device, and that many do for some device. `edge_src`: every edge of a device has its source pair on that same device. `edge_dst`: an edge's target pair lies in the same group as its source, on another device; of one device's edges at most 4 end on pairs of any one other device, and at most 4 have the mirror of their target pair on any one device (that device itself included); both bounds are reached on some device. `amps`: mirror pairs hold transposed tiles. `ints`: mirror pairs hold transposed tiles. `pno_energy`: mirror pairs hold equal rows.
All inputs are finite; a program needn't handle non-finite values.
Results may differ from the reference program's by a relative error of at most 0.0065.
Values may be sent and summed in bfloat16 or wider, within the bound.
A program may use at most 64 MiB of HBM per device.

```python
import jax
import jax.numpy as jnp
from jax import lax

RANK = 128
NOCC = 1000
PAIR_DEV = 28
EDGE_DEV = 48
PAIRS = 896
EDGES = 1536
N_GRP = 2
N_OWN = 16


def owner_labels(key):
    labels = jax.vmap(lambda sub_key: jax.random.permutation(sub_key, N_OWN))(jax.random.split(key, N_GRP)).astype(jnp.int32)
    inverse = jnp.argsort(labels, axis=1).astype(jnp.int32)
    values = jax.vmap(lambda sub_key: jax.random.permutation(sub_key, N_OWN - 1))(jax.random.split(jax.random.fold_in(key, 5), N_GRP)).astype(jnp.int32) + 1
    return (labels, inverse, values)


def couple_structure(key):
    labels, inverse, values = owner_labels(jax.random.fold_in(key, 1))
    rounds = jnp.arange(PAIR_DEV) % (N_OWN - 1)
    xor_round = values[:, rounds]
    partner_label = jnp.bitwise_xor(labels[:, :, None], xor_round[:, None, :])
    partner = jax.vmap(lambda inverse_row, label_row: inverse_row[label_row])(inverse, partner_label)
    leader = labels[:, :, None] < partner_label
    slot_keys = jax.random.split(jax.random.fold_in(key, 2), N_GRP * N_OWN)
    slot_round = jax.vmap(lambda sub_key: jax.random.permutation(sub_key, PAIR_DEV))(slot_keys).astype(jnp.int32).reshape(N_GRP, N_OWN, PAIR_DEV)
    round_slot = jnp.argsort(slot_round, axis=2).astype(jnp.int32)
    groups = jnp.arange(N_GRP, dtype=jnp.int32)[:, None, None]
    owners = jnp.arange(N_OWN, dtype=jnp.int32)[None, :, None]
    part_at = jnp.take_along_axis(partner, slot_round, axis=2)
    lead_at = jnp.take_along_axis(leader, slot_round, axis=2)
    mirror_slot = round_slot[groups, part_at, slot_round]
    mirror = (groups * N_OWN + part_at) * PAIR_DEV + mirror_slot
    lead_owner = jnp.where(lead_at, owners, part_at)
    content = (groups * N_OWN + lead_owner) * PAIR_DEV + slot_round
    return (mirror.reshape(-1).astype(jnp.int32), lead_at.reshape(-1), content.reshape(-1).astype(jnp.int32), labels, inverse, values, round_slot)


def couple_layout(key):
    mirror, lead_flag, content, labels, inverse, values, round_slot = couple_structure(key)
    return (mirror, lead_flag, content)


def couple_tiles(key, base_table):
    mirror, lead_flag, content = couple_layout(jax.random.fold_in(key, 101))
    picked = base_table[content]
    return jnp.where(lead_flag[:, None, None], picked, jnp.swapaxes(picked, 1, 2))


def draw_amps(key, part):
    jitter = jax.random.normal(jax.random.fold_in(key, 7), (PAIRS, RANK, RANK), jnp.float32)
    base_table = jnp.clip(0.07 * jitter, -0.35, 0.35)
    return couple_tiles(key, base_table).astype(jnp.bfloat16)


def draw_ints(key, part):
    jitter = jax.random.normal(jax.random.fold_in(key, 8), (PAIRS, RANK, RANK), jnp.float32)
    base_table = jnp.clip(0.1 * jitter, -0.5, 0.5)
    return couple_tiles(key, base_table).astype(jnp.bfloat16)


def draw_pno_energy(key, part):
    mirror, lead_flag, content = couple_layout(jax.random.fold_in(key, 101))
    base_table = jax.random.uniform(jax.random.fold_in(key, 12), (PAIRS, RANK), jnp.float32, 0.2, 2.0)
    return base_table[content]


def draw_pair_occ(key, part):
    mirror, lead_flag, content = couple_layout(jax.random.fold_in(key, 101))
    first_occ = jax.random.randint(jax.random.fold_in(key, 9), (PAIRS,), 0, NOCC)
    offset = jax.random.randint(jax.random.fold_in(key, 10), (PAIRS,), 1, NOCC)
    second_occ = (first_occ + offset) % NOCC
    first_moved = first_occ[content]
    second_moved = second_occ[content]
    occ_left = jnp.where(lead_flag, first_moved, second_moved)
    occ_right = jnp.where(lead_flag, second_moved, first_moved)
    return jnp.stack([occ_left, occ_right]).astype(jnp.int32)


def draw_mirror(key, part):
    mirror, lead_flag, content = couple_layout(jax.random.fold_in(key, 101))
    return mirror


def edge_layout(key):
    mirror, lead_flag, content, labels, inverse, values, round_slot = couple_structure(jax.random.fold_in(key, 101))
    edge_key = jax.random.fold_in(key, 202)
    order_keys = jax.random.split(jax.random.fold_in(edge_key, 3), N_GRP * N_OWN)
    order = jax.vmap(lambda sub_key: jax.random.permutation(sub_key, N_OWN - 1))(order_keys).astype(jnp.int32).reshape(N_GRP, N_OWN, N_OWN - 1)
    own_round = jax.random.randint(jax.random.fold_in(edge_key, 4), (N_GRP, N_OWN), 0, PAIR_DEV).astype(jnp.int32)
    shift_val = jnp.take_along_axis(values, own_round % (N_OWN - 1), axis=1)
    cycle_pos = jnp.arange(EDGE_DEV) % (N_OWN - 1)
    picked = order[:, :, cycle_pos]
    offset = picked + (picked >= shift_val[:, :, None]).astype(jnp.int32)
    target_label = jnp.bitwise_xor(jnp.bitwise_xor(labels[:, :, None], offset), shift_val[:, :, None])
    target_owner = jax.vmap(lambda inverse_row, label_row: inverse_row[label_row])(inverse, target_label)
    groups = jnp.arange(N_GRP, dtype=jnp.int32)[:, None, None]
    owners = jnp.arange(N_OWN, dtype=jnp.int32)[None, :, None]
    target_slot = round_slot[groups, target_owner, own_round[:, :, None]]
    source_slot = jax.random.randint(jax.random.fold_in(edge_key, 6), (N_GRP, N_OWN, EDGE_DEV), 0, PAIR_DEV).astype(jnp.int32)
    target = (groups * N_OWN + target_owner) * PAIR_DEV + target_slot
    source = (groups * N_OWN + owners) * PAIR_DEV + source_slot
    return (source.reshape(-1).astype(jnp.int32), target.reshape(-1).astype(jnp.int32))


def draw_edge_src(key, part):
    source, target = edge_layout(key)
    return source


def draw_edge_dst(key, part):
    source, target = edge_layout(key)
    return target


def draw_margin(key, part):
    diag_part = jax.random.uniform(jax.random.fold_in(key, 21), (EDGES, RANK), jnp.float32, 0.6, 1.0)
    jitter = jax.random.normal(jax.random.fold_in(key, 22), (EDGES, RANK, RANK), jnp.float32) * 0.03
    jitter = jnp.clip(jitter, -0.12, 0.12)
    return (jitter + diag_part[:, :, None] * jnp.eye(RANK, dtype=jnp.float32)[None]).astype(jnp.bfloat16)


def shard_levels(stream_key, extent, cuts, low, high):
    def one(axis_at, blocks):
        heights = jax.random.uniform(jax.random.fold_in(jax.random.fold_in(stream_key, 6), axis_at), (blocks,), jnp.float32, low / len(cuts), high / len(cuts))
        return jnp.repeat(jnp.exp(heights), extent[axis_at] // blocks).reshape((-1,) + (1,) * (len(extent) - axis_at - 1))

    loudness = one(*cuts[0])
    for cut in cuts[1:]:
        loudness = loudness * one(*cut)
    return loudness


def setup_inputs(seed: int = 0) -> dict:
    splits = jax.random.split(jax.random.key(seed), 11)
    amps = draw_amps(jax.random.fold_in(splits[10], 71), 0)
    ints = draw_ints(jax.random.fold_in(splits[10], 71), 0)
    pno_energy = draw_pno_energy(jax.random.fold_in(splits[10], 71), 0)
    occ_energy = jnp.clip(jax.random.uniform(splits[3], (NOCC,), jnp.float32, -1.0, -0.2), -1.0, -0.2)
    pair_occ = draw_pair_occ(jax.random.fold_in(splits[10], 71), 0)
    mirror = draw_mirror(jax.random.fold_in(splits[10], 71), 0)
    edge_src = draw_edge_src(jax.random.fold_in(splits[10], 71), 0)
    edge_dst = draw_edge_dst(jax.random.fold_in(splits[10], 71), 0)
    edge_fock = jnp.clip(jax.random.uniform(splits[8], (EDGES,), jnp.float32, -6.0, 6.0) * shard_levels(splits[8], (EDGES,), ((0, 32),), -0.4, 0.0), -6.0, 6.0)
    margin = draw_margin(jax.random.fold_in(splits[10], 71), 0)
    return {"amps": amps, "ints": ints, "pno_energy": pno_energy, "occ_energy": occ_energy, "pair_occ": pair_occ, "mirror": mirror, "edge_src": edge_src, "edge_dst": edge_dst, "edge_fock": edge_fock, "margin": margin}


def reference(amps, ints, pno_energy, occ_energy, pair_occ, mirror, edge_src, edge_dst, edge_fock, margin):
    amp_f32 = amps.astype(jnp.float32)
    int_f32 = ints.astype(jnp.float32)
    pair_energy = jnp.sum((2.0 * int_f32 - jnp.swapaxes(int_f32, 1, 2)) * amp_f32, axis=(1, 2))
    first_occ = pair_occ[0].astype(jnp.int32)
    second_occ = pair_occ[1].astype(jnp.int32)
    occ_sum = jnp.zeros((NOCC,), jnp.float32).at[first_occ].add(pair_energy)
    cepa_shift = 0.5 * (occ_sum[first_occ] + occ_sum[second_occ])
    fock_pair = occ_energy[first_occ] + occ_energy[second_occ]
    diagonal = (pno_energy[:, :, None] + pno_energy[:, None, :] - fock_pair[:, None, None]) - cepa_shift[:, None, None]
    local_part = 0.5 * int_f32 + diagonal * amp_f32

    blocks = EDGES // EDGE_DEV

    def project(inputs):
        source_ids, margin_block, fock_row = inputs
        source_tiles = jnp.take(amps, source_ids, axis=0).astype(jnp.float32)
        margin_f32 = margin_block.astype(jnp.float32)
        projected = jnp.einsum("eab,ebc->eac", margin_f32, source_tiles).astype(jnp.bfloat16)
        product = jnp.einsum("eab,ecb->eac", projected.astype(jnp.float32), margin_f32)
        return (product * fock_row[:, None, None]).astype(jnp.bfloat16)

    coupled = lax.map(project, (edge_src.reshape(blocks, EDGE_DEV), margin.reshape(blocks, EDGE_DEV, RANK, RANK), edge_fock.reshape(blocks, EDGE_DEV)))
    coupled = coupled.reshape(EDGES, RANK, RANK)
    coupling = jnp.zeros((PAIRS, RANK, RANK), jnp.float32).at[edge_dst].add(coupled.astype(jnp.float32))
    half_res = (local_part + coupling).astype(jnp.bfloat16)
    partner = jnp.swapaxes(jnp.take(half_res, mirror, axis=0), 1, 2)
    return (half_res.astype(jnp.float32) + partner.astype(jnp.float32)).astype(jnp.bfloat16)
```

```python
import functools

import jax
import jax.numpy as jnp
from jax import lax
from jax.experimental import pallas as pl
from jax.experimental.pallas import tpu as pltpu
from jax.sharding import PartitionSpec as P

MESH = pl.DeviceIdType.MESH
LANES = 128
EARLY_STEPS = 4


def step_offset(step, devices):
    half = (step + 1) // 2
    signed = jnp.where(step % 2 == 1, devices - 1 - half, half)
    return 1 + lax.rem(devices // 2 - 1 + signed, devices - 1)


def kernel(
    dims,
    ids,
    scales,
    amps,
    ints,
    pno,
    margin,
    out,
    send_edge,
    recv_edge,
    running,
    local_part,
    send_half,
    recv_half,
    flipped,
    grp_sums,
    own_sums,
    edge_send_sem,
    edge_recv_sem,
    half_send_sem,
    half_recv_sem,
    grp_send_sem,
    grp_recv_sem,
    own_send_sem,
    own_recv_sem,
):
    groups, owners, pairs, edge_cap, mirror_cap, occ_rows = dims
    edge_slots = owners * edge_cap
    half_slots = owners * mirror_cap
    rank = amps.shape[1]
    group = lax.axis_index("grp")
    me = lax.axis_index("own")

    at_edge, at_src, at_order = 0, edge_slots, 2 * edge_slots
    at_last = 3 * edge_slots
    at_first, at_second = at_last + pairs, at_last + 2 * pairs
    at_pack = at_last + 3 * pairs
    at_in = at_pack + half_slots
    at_out = at_in + pairs
    at_keep, at_has = edge_slots, 2 * edge_slots
    at_fock = at_has + pairs

    barrier = pltpu.get_barrier_semaphore()

    @pl.loop(1, owners)
    def _(offset):
        pl.semaphore_signal(
            barrier,
            inc=1,
            device_id=(group, lax.rem(me + offset, owners)),
            device_id_type=MESH,
        )

    @pl.loop(1, groups)
    def _(offset):
        pl.semaphore_signal(
            barrier,
            inc=1,
            device_id=(lax.rem(group + offset, groups), me),
            device_id_type=MESH,
        )

    pl.semaphore_wait(barrier, owners + groups - 2)

    def edge_copy(offset):
        target = lax.rem(me + offset, owners)
        return pltpu.make_async_remote_copy(
            src_ref=send_edge.at[pl.ds(target * edge_cap, edge_cap)],
            dst_ref=recv_edge.at[pl.ds(me * edge_cap, edge_cap)],
            send_sem=edge_send_sem.at[offset],
            recv_sem=edge_recv_sem.at[offset],
            device_id=(group, target),
            device_id_type=MESH,
        )

    def half_copy(offset):
        target = lax.rem(me + offset, owners)
        return pltpu.make_async_remote_copy(
            src_ref=send_half.at[pl.ds(target * mirror_cap, mirror_cap)],
            dst_ref=recv_half.at[pl.ds(me * mirror_cap, mirror_cap)],
            send_sem=half_send_sem.at[offset],
            recv_sem=half_recv_sem.at[offset],
            device_id=(group, target),
            device_id_type=MESH,
        )

    def grp_copy(offset):
        return pltpu.make_async_remote_copy(
            src_ref=grp_sums.at[group],
            dst_ref=grp_sums.at[group],
            send_sem=grp_send_sem.at[offset],
            recv_sem=grp_recv_sem.at[offset],
            device_id=(lax.rem(group + offset, groups), me),
            device_id_type=MESH,
        )

    def own_copy(offset):
        return pltpu.make_async_remote_copy(
            src_ref=own_sums.at[me],
            dst_ref=own_sums.at[me],
            send_sem=own_send_sem.at[offset],
            recv_sem=own_recv_sem.at[offset],
            device_id=(group, lax.rem(me + offset, owners)),
            device_id_type=MESH,
        )

    def send_step(step):
        offset = step_offset(step, owners)
        target = lax.rem(me + offset, owners)
        for k in range(edge_cap):
            slot = target * edge_cap + k
            tile = margin[ids[at_edge + slot]]
            projected = jnp.dot(
                tile, amps[ids[at_src + slot]], preferred_element_type=jnp.float32
            ).astype(jnp.bfloat16)
            product = lax.dot_general(
                projected, tile, (((1,), (1,)), ((), ())), preferred_element_type=jnp.float32
            )
            send_edge[slot] = (product * scales[slot]).astype(jnp.bfloat16)
        edge_copy(offset).start()

    early = min(EARLY_STEPS, owners - 1)
    pl.loop(0, early)(send_step)

    rows = lax.broadcasted_iota(jnp.int32, (rank, rank), 0)
    columns = lax.broadcasted_iota(jnp.int32, (rank, rank), 1)
    on_diagonal = rows == columns
    occ_ids = lax.broadcasted_iota(
        jnp.int32, (occ_rows, LANES), 0
    ) * LANES + lax.broadcasted_iota(jnp.int32, (occ_rows, LANES), 1)

    def add_energy(p, partial):
        int_tile, amp_tile = ints[p], amps[p]
        product = jnp.dot(int_tile, amp_tile, preferred_element_type=jnp.float32)
        direct = 2.0 * int_tile.astype(jnp.float32) * amp_tile.astype(jnp.float32)
        terms = direct - jnp.where(on_diagonal, product, 0.0)
        energy = jnp.sum(jnp.sum(terms, axis=0, keepdims=True), axis=1, keepdims=True)
        return partial + jnp.where(occ_ids == ids[at_first + p], energy, 0.0)

    partial = lax.fori_loop(0, pairs, add_energy, jnp.zeros((occ_rows, LANES), jnp.float32))
    grp_sums[group] = partial

    @pl.loop(1, groups)
    def _(offset):
        grp_copy(offset).start()

    pl.loop(early, owners - 1)(send_step)

    @pl.loop(1, groups)
    def _(offset):
        grp_copy(offset).wait()

    own_sums[me] = jnp.sum(grp_sums[...], axis=0)

    @pl.loop(1, owners)
    def _(offset):
        own_copy(offset).start()

    for k in range(edge_cap):
        recv_edge[me * edge_cap + k] = jnp.zeros((rank, rank), jnp.bfloat16)

    @pl.loop(1, owners)
    def _(offset):
        own_copy(offset).wait()

    occ_sum = jnp.sum(own_sums[...], axis=0)

    @pl.loop(0, pairs)
    def _(p):
        hits = jnp.where(occ_ids == ids[at_first + p], occ_sum, 0.0) + jnp.where(
            occ_ids == ids[at_second + p], occ_sum, 0.0
        )
        shift = 0.5 * jnp.sum(jnp.sum(hits, axis=0, keepdims=True), axis=1, keepdims=True)
        across = jnp.broadcast_to(pno[p], (rank, rank))
        diagonal = ((across + across.T) - scales[at_fock + p]) - shift
        local_part[p] = 0.5 * ints[p].astype(jnp.float32) + diagonal * amps[p].astype(jnp.float32)

    @pl.loop(1, owners)
    def _(offset):
        edge_copy(offset).wait()

    def accumulate(j, total):
        total = total * scales[at_keep + j] + recv_edge[ids[at_order + j]].astype(jnp.float32)
        running[j] = total
        return total

    lax.fori_loop(0, edge_slots, accumulate, jnp.zeros((rank, rank), jnp.float32))

    @pl.loop(0, owners - 1)
    def _(step):
        offset = step_offset(step, owners)
        target = lax.rem(me + offset, owners)
        for k in range(mirror_cap):
            slot = target * mirror_cap + k
            p = ids[at_pack + slot]
            coupling = running[ids[at_last + p]] * scales[at_has + p]
            send_half[slot] = (local_part[p] + coupling).astype(jnp.bfloat16)
        half_copy(offset).start()

    @pl.loop(0, owners - 1)
    def _(step):
        offset = step_offset(step, owners)
        half_copy(offset).wait_recv()
        sender = lax.rem(me - offset + owners, owners)
        for k in range(mirror_cap):
            slot = sender * mirror_cap + k
            flipped[slot] = recv_half[slot].astype(jnp.float32).T

    @pl.loop(0, pairs)
    def _(p):
        own_tile = send_half[ids[at_out + p]].astype(jnp.float32)
        out[p] = (own_tile + flipped[ids[at_in + p]]).astype(jnp.bfloat16)

    @pl.loop(1, owners)
    def _(offset):
        half_copy(offset).wait_send()


def local(
    amps, ints, pno_energy, occ_energy, pair_occ, mirror, edge_src, edge_dst, edge_fock, margin
):
    groups = lax.axis_size("grp")
    owners = lax.axis_size("own")
    my_owner = lax.axis_index("own")
    group_index = lax.axis_index("grp")
    pairs = amps.shape[0]
    rank = amps.shape[1]
    edge_count = edge_src.shape[0]
    occ_count = occ_energy.shape[0]
    mirror_cap = (pairs + owners - 2) // (owners - 1)
    edge_cap = (edge_count + owners - 2) // (owners - 1)
    edge_slots = owners * edge_cap
    half_slots = owners * mirror_cap
    group_base = group_index * (owners * pairs)
    device_base = group_base + my_owner * pairs
    iota = functools.partial(lax.iota, jnp.int32)

    group_dst = edge_dst - group_base
    dst_owner = group_dst // pairs
    dst_slot = group_dst % pairs
    mine = lax.dynamic_slice_in_dim(dst_owner, my_owner * edge_count, edge_count)
    earlier = iota(edge_count)[None, :] < iota(edge_count)[:, None]
    place = mine * edge_cap + jnp.sum(
        ((mine[:, None] == mine[None, :]) & earlier).astype(jnp.int32), axis=1
    )
    placed = place[None, :] == iota(edge_slots)[:, None]
    slot_edge = jnp.sum(jnp.where(placed, iota(edge_count)[None, :], 0), axis=1)
    slot_src = jnp.sum(jnp.where(placed, (edge_src - device_base)[None, :], 0), axis=1)
    slot_fock = jnp.sum(jnp.where(placed, edge_fock[None, :], 0.0), axis=1)

    owner_rows = dst_owner.reshape(owners, edge_count)
    arriving = owner_rows == my_owner
    rank_rows = jnp.sum(
        (arriving[:, None, :] & earlier[None, :, :]).astype(jnp.int32), axis=2
    )
    here = arriving[:, :, None] & (rank_rows[:, :, None] == iota(edge_cap)[None, None, :])
    slot_rows = dst_slot.reshape(owners, edge_count)[:, :, None] - pairs
    arrived_dst = (jnp.sum(jnp.where(here, slot_rows, 0), axis=1) + pairs).reshape(-1)
    sort_key = arrived_dst * edge_slots + iota(edge_slots)
    position = jnp.sum((sort_key[None, :] < sort_key[:, None]).astype(jnp.int32), axis=1)
    sorted_hit = position[None, :] == iota(edge_slots)[:, None]
    order = jnp.sum(jnp.where(sorted_hit, iota(edge_slots)[None, :], 0), axis=1)
    sorted_dst = jnp.sum(jnp.where(sorted_hit, arrived_dst[None, :], 0), axis=1)
    keep = jnp.concatenate(
        [jnp.zeros((1,), jnp.float32), (sorted_dst[1:] == sorted_dst[:-1]).astype(jnp.float32)]
    )
    pair_ids = iota(pairs)
    up_to = jnp.sum((arrived_dst[None, :] <= pair_ids[:, None]).astype(jnp.int32), axis=1)
    last = jnp.maximum(up_to - 1, 0)
    has = jnp.max((arrived_dst[None, :] == pair_ids[:, None]).astype(jnp.float32), axis=1)

    mirror_local = mirror - group_base
    mirror_owner = mirror_local // pairs
    mirror_slot = mirror_local % pairs
    same_owner = mirror_owner[:, None] == mirror_owner[None, :]
    out_rank = jnp.sum(
        (same_owner & (pair_ids[None, :] < pair_ids[:, None])).astype(jnp.int32), axis=1
    )
    in_rank = jnp.sum(
        (same_owner & (mirror_slot[None, :] < mirror_slot[:, None])).astype(jnp.int32), axis=1
    )
    out_place = mirror_owner * mirror_cap + out_rank
    in_place = mirror_owner * mirror_cap + in_rank
    pack = jnp.sum(
        jnp.where(out_place[None, :] == iota(half_slots)[:, None], pair_ids[None, :], 0), axis=1
    )

    occ_ids = iota(occ_count)
    occ_hit = (pair_occ[0][:, None] == occ_ids[None, :]).astype(jnp.float32) + (
        pair_occ[1][:, None] == occ_ids[None, :]
    ).astype(jnp.float32)
    fock_pair = jnp.sum(occ_hit * occ_energy[None, :], axis=1)

    ids = jnp.concatenate(
        [slot_edge, slot_src, order, last, pair_occ[0], pair_occ[1], pack, in_place, out_place]
    )
    scales = jnp.concatenate([slot_fock, keep, has, fock_pair])

    occ_rows = -(-occ_count // LANES)
    dims = (groups, owners, pairs, edge_cap, mirror_cap, occ_rows)
    vmem = pl.BlockSpec(memory_space=pltpu.VMEM)
    smem = pl.BlockSpec(memory_space=pltpu.SMEM)
    dma = pltpu.SemaphoreType.DMA
    return pl.pallas_call(
        functools.partial(kernel, dims),
        out_shape=jax.ShapeDtypeStruct(amps.shape, jnp.bfloat16),
        in_specs=[smem, smem, vmem, vmem, vmem, vmem],
        out_specs=vmem,
        scratch_shapes=[
            pltpu.VMEM((edge_slots, rank, rank), jnp.bfloat16),
            pltpu.VMEM((edge_slots, rank, rank), jnp.bfloat16),
            pltpu.VMEM((edge_slots, rank, rank), jnp.float32),
            pltpu.VMEM((pairs, rank, rank), jnp.float32),
            pltpu.VMEM((half_slots, rank, rank), jnp.bfloat16),
            pltpu.VMEM((half_slots, rank, rank), jnp.bfloat16),
            pltpu.VMEM((half_slots, rank, rank), jnp.float32),
            pltpu.VMEM((groups, occ_rows, LANES), jnp.float32),
            pltpu.VMEM((owners, occ_rows, LANES), jnp.float32),
            dma((owners,)),
            dma((owners,)),
            dma((owners,)),
            dma((owners,)),
            dma((groups,)),
            dma((groups,)),
            dma((owners,)),
            dma((owners,)),
        ],
        compiler_params=pltpu.CompilerParams(
            collective_id=0, has_side_effects=True, vmem_limit_bytes=56 * 1024 * 1024
        ),
    )(ids, scales, amps, ints, pno_energy.reshape(pairs, 1, rank), margin)


def solution(mesh):
    in_specs = (
        P(("grp", "own"), None, None),
        P(("grp", "own"), None, None),
        P(("grp", "own"), None),
        P(),
        P(None, ("grp", "own")),
        P(("grp", "own")),
        P(("grp", "own")),
        P("grp"),
        P(("grp", "own")),
        P(("grp", "own"), None, None),
    )
    out_specs = P(("grp", "own"), None, None)
    return jax.shard_map(local, mesh=mesh, in_specs=in_specs, out_specs=out_specs, check_vma=False)
```

```python
import functools

import jax
import jax.numpy as jnp
from jax import lax
from jax.experimental import pallas as pl
from jax.experimental.pallas import tpu as pltpu
from jax.sharding import PartitionSpec as P

MESH = pl.DeviceIdType.MESH
LANES = 128
EARLY_STEPS = 4


def step_offset(step, devices):
    spread = jnp.where(step % 2 == 1, devices - 2 - step // 2, step // 2)
    half = (spread + 1) // 2
    signed = jnp.where(spread % 2 == 1, devices - 1 - half, half)
    return 1 + lax.rem(devices // 2 - 1 + signed, devices - 1)


def within(index, size):
    return jnp.minimum(jnp.maximum(index, 0), size - 1)


def kernel(
    dims,
    occ,
    occ_energy,
    mirror,
    edge_src,
    edge_dst,
    edge_fock,
    pno,
    amps,
    ints,
    margin,
    out,
    send_edge,
    recv_edge,
    running,
    local_part,
    send_half,
    recv_half,
    flipped,
    grp_sums,
    own_sums,
    table,
    early_rows,
    early_scale_rows,
    late_rows,
    late_scale_rows,
    early,
    early_scales,
    late,
    late_scales,
    table_sem,
    edge_send_sem,
    edge_recv_sem,
    half_send_sem,
    half_recv_sem,
    grp_send_sem,
    grp_recv_sem,
    own_send_sem,
    own_recv_sem,
):
    groups, owners, pairs, edge_cap, mirror_cap, occ_rows = dims
    edge_slots = owners * edge_cap
    half_slots = owners * mirror_cap
    rank = amps.shape[1]
    group = lax.axis_index("grp")
    me = lax.axis_index("own")

    width = table.shape[1]
    at_slot, at_src, at_fock = owners, 2 * owners, 2 * owners + 1
    at_partner, at_place = 2 * owners + 2, 2 * owners + 3
    at_occ = 2 * owners + 4
    edge_count = edge_src.shape[1]
    occ_count = occ_energy.shape[1]

    barrier = pltpu.get_barrier_semaphore()

    @pl.loop(1, owners)
    def _(offset):
        pl.semaphore_signal(
            barrier,
            inc=1,
            device_id=(group, lax.rem(me + offset, owners)),
            device_id_type=MESH,
        )

    @pl.loop(1, groups)
    def _(offset):
        pl.semaphore_signal(
            barrier,
            inc=1,
            device_id=(lax.rem(group + offset, groups), me),
            device_id_type=MESH,
        )

    down = lax.broadcasted_iota(jnp.int32, (width, width), 0)
    right = lax.broadcasted_iota(jnp.int32, (width, width), 1)
    down_f, right_f = down.astype(jnp.float32), right.astype(jnp.float32)

    group_base = (group * (owners * pairs)).astype(jnp.float32)
    device_base = group_base + (me * pairs).astype(jnp.float32)

    def owner_and_slot(pair):
        at = pair.astype(jnp.float32) - group_base
        owner = jnp.floor((at + 0.5) / pairs)
        return owner, at - owner * pairs

    table[0:owners, :] = jnp.full((owners, width), -1.0, jnp.float32)
    table[owners:, :] = jnp.zeros((table.shape[0] - owners, width), jnp.float32)
    table[at_partner : at_partner + 1, :] = jnp.full((1, width), -1.0, jnp.float32)
    dst_owner, dst_slot = owner_and_slot(edge_dst[...])
    for o in range(owners):
        span = slice(o * edge_count, (o + 1) * edge_count)
        table[o : o + 1, 0:edge_count] = dst_owner[:, span]
        table[at_slot + o : at_slot + o + 1, 0:edge_count] = dst_slot[:, span]
    table[at_src : at_src + 1, 0:edge_count] = edge_src[...].astype(jnp.float32) - device_base
    table[at_fock : at_fock + 1, 0:edge_count] = edge_fock[...]
    partner, spot = owner_and_slot(mirror[...])
    table[at_partner : at_partner + 1, 0:pairs] = partner
    table[at_place : at_place + 1, 0:pairs] = spot
    for r in range(occ_rows):
        count = min(LANES, occ_count - r * LANES)
        table[at_occ + r : at_occ + r + 1, 0:count] = occ_energy[:, r * LANES : r * LANES + count]

    def along(row):
        return jnp.broadcast_to(table[pl.ds(row, 1), :], (width, width))

    def count_down(mask):
        return jnp.sum(jnp.where(mask, 1.0, 0.0), axis=0, keepdims=True)

    def count_right(mask):
        return jnp.sum(jnp.where(mask, 1.0, 0.0), axis=1, keepdims=True)

    def pick_down(mask, values):
        return jnp.sum(jnp.where(mask, values, 0.0), axis=0, keepdims=True)

    to_right = along(me)
    to_down = to_right.T
    nth = count_right((to_down == to_right) & (right < down))
    fills = (to_down * edge_cap + nth == right_f) & (to_down >= 0.0)
    early_rows[0:1, :] = pick_down(fills, down_f).astype(jnp.int32)
    early_rows[1:2, :] = pick_down(fills, along(at_src).T).astype(jnp.int32)
    early_rows[2:8, :] = jnp.zeros((6, width), jnp.int32)
    early_scale_rows[...] = jnp.broadcast_to(pick_down(fills, along(at_fock).T), (8, width))
    to_early = pltpu.make_async_copy(early_rows, early, table_sem.at[0])
    to_early_scales = pltpu.make_async_copy(early_scale_rows, early_scales, table_sem.at[1])
    to_early.start()
    to_early_scales.start()
    to_early.wait()
    to_early_scales.wait()

    pl.semaphore_wait(barrier, owners + groups - 2)

    def edge_copy(offset):
        target = lax.rem(me + offset, owners)
        return pltpu.make_async_remote_copy(
            src_ref=send_edge.at[pl.ds(target * edge_cap, edge_cap)],
            dst_ref=recv_edge.at[pl.ds(me * edge_cap, edge_cap)],
            send_sem=edge_send_sem.at[offset],
            recv_sem=edge_recv_sem.at[offset],
            device_id=(group, target),
            device_id_type=MESH,
        )

    def half_copy(offset):
        target = lax.rem(me + offset, owners)
        return pltpu.make_async_remote_copy(
            src_ref=send_half.at[pl.ds(target * mirror_cap, mirror_cap)],
            dst_ref=recv_half.at[pl.ds(me * mirror_cap, mirror_cap)],
            send_sem=half_send_sem.at[offset],
            recv_sem=half_recv_sem.at[offset],
            device_id=(group, target),
            device_id_type=MESH,
        )

    def grp_copy(offset):
        return pltpu.make_async_remote_copy(
            src_ref=grp_sums.at[group],
            dst_ref=grp_sums.at[group],
            send_sem=grp_send_sem.at[offset],
            recv_sem=grp_recv_sem.at[offset],
            device_id=(lax.rem(group + offset, groups), me),
            device_id_type=MESH,
        )

    def own_copy(offset):
        return pltpu.make_async_remote_copy(
            src_ref=own_sums.at[me],
            dst_ref=own_sums.at[me],
            send_sem=own_send_sem.at[offset],
            recv_sem=own_recv_sem.at[offset],
            device_id=(group, lax.rem(me + offset, owners)),
            device_id_type=MESH,
        )

    def send_step(step):
        offset = step_offset(step, owners)
        target = lax.rem(me + offset, owners)
        for k in range(edge_cap):
            slot = target * edge_cap + k
            tile = margin[within(early[0, slot], margin.shape[0])]
            projected = jnp.dot(
                tile, amps[within(early[1, slot], pairs)], preferred_element_type=jnp.float32
            ).astype(jnp.bfloat16)
            product = lax.dot_general(
                projected, tile, (((1,), (1,)), ((), ())), preferred_element_type=jnp.float32
            )
            send_edge[slot] = (product * early_scales[0, slot]).astype(jnp.bfloat16)
        edge_copy(offset).start()

    first = min(EARLY_STEPS, owners - 1)
    pl.loop(0, first)(send_step)

    rows = lax.broadcasted_iota(jnp.int32, (rank, rank), 0)
    columns = lax.broadcasted_iota(jnp.int32, (rank, rank), 1)
    on_diagonal = rows == columns
    occ_ids = lax.broadcasted_iota(
        jnp.int32, (occ_rows, LANES), 0
    ) * LANES + lax.broadcasted_iota(jnp.int32, (occ_rows, LANES), 1)

    def add_energy(p, partial):
        int_tile, amp_tile = ints[p], amps[p]
        product = jnp.dot(int_tile, amp_tile, preferred_element_type=jnp.float32)
        direct = 2.0 * int_tile.astype(jnp.float32) * amp_tile.astype(jnp.float32)
        terms = direct - jnp.where(on_diagonal, product, 0.0)
        energy = jnp.sum(jnp.sum(terms, axis=0, keepdims=True), axis=1, keepdims=True)
        return partial + jnp.where(occ_ids == occ[0, p], energy, 0.0)

    partial = lax.fori_loop(0, pairs, add_energy, jnp.zeros((occ_rows, LANES), jnp.float32))
    grp_sums[group] = partial

    @pl.loop(1, groups)
    def _(offset):
        grp_copy(offset).start()

    pl.loop(first, owners - 1)(send_step)

    @pl.loop(1, groups)
    def _(offset):
        grp_copy(offset).wait()

    own_sums[me] = jnp.sum(grp_sums[...], axis=0)

    @pl.loop(1, owners)
    def _(offset):
        own_copy(offset).start()

    for k in range(edge_cap):
        recv_edge[me * edge_cap + k] = jnp.zeros((rank, rank), jnp.bfloat16)

    arriving = table[0:owners, :] == me.astype(jnp.float32)
    before = jnp.dot(
        jnp.where(arriving, 1.0, 0.0).astype(jnp.bfloat16),
        jnp.where(down < right, 1.0, 0.0).astype(jnp.bfloat16),
        preferred_element_type=jnp.float32,
    )
    ends = table[at_slot : at_slot + owners, :] - pairs
    blocks = [
        jnp.broadcast_to(
            jnp.sum(jnp.where(arriving & (before == k), ends, 0.0), axis=1, keepdims=True) + pairs,
            (owners, width),
        )
        for k in range(edge_cap)
    ]
    if width > edge_slots:
        blocks.append(jnp.full((width - edge_slots, width), pairs, jnp.float32))
    end_down = jnp.concatenate(blocks, axis=0)
    end_right = end_down.T
    place = count_right((end_right < end_down) | ((end_right == end_down) & (right < down)))
    sender = lax.rem(down, owners)
    slot_down = (sender * edge_cap + lax.div(down, owners)).astype(jnp.float32)
    at_place_now = place == right_f
    order = pick_down(at_place_now, slot_down)
    sorted_end = pick_down(at_place_now, end_down)
    previous_end = pick_down(place + 1.0 == right_f, end_down)
    last = jnp.maximum(count_down(end_down <= right_f) - 1.0, 0.0)

    partner_right = along(at_partner)
    partner_down = partner_right.T
    spot_right = along(at_place)
    same = (partner_right == partner_down) & (partner_right >= 0.0)
    out_place = partner_right * mirror_cap + count_down(same & (down < right))
    in_place = partner_right * mirror_cap + count_down(same & (spot_right.T < spot_right))
    out_down = partner_down * mirror_cap + count_right(same & (right < down))
    packed = pick_down((out_down == right_f) & (partner_down >= 0.0), down_f)

    for row, values in enumerate(
        (order, last, packed, jnp.maximum(in_place[0:1], 0.0), jnp.maximum(out_place[0:1], 0.0))
    ):
        late_rows[row : row + 1, :] = values.astype(jnp.int32)
    late_rows[5:8, :] = jnp.zeros((3, width), jnp.int32)
    late_scale_rows[0:1, :] = jnp.where(sorted_end == previous_end, 1.0, 0.0)
    late_scale_rows[1:2, :] = jnp.minimum(count_down(end_down == right_f), 1.0)
    late_scale_rows[2:8, :] = jnp.zeros((6, width), jnp.float32)
    to_late = pltpu.make_async_copy(late_rows, late, table_sem.at[2])
    to_late_scales = pltpu.make_async_copy(late_scale_rows, late_scales, table_sem.at[3])
    to_late.start()
    to_late_scales.start()
    to_late.wait()
    to_late_scales.wait()

    @pl.loop(1, owners)
    def _(offset):
        own_copy(offset).wait()

    occ_terms = table[at_occ : at_occ + occ_rows, :LANES] + 0.5 * jnp.sum(own_sums[...], axis=0)

    @pl.loop(0, pairs)
    def _(p):
        hits = jnp.where(occ_ids == occ[0, p], occ_terms, 0.0) + jnp.where(
            occ_ids == occ[1, p], occ_terms, 0.0
        )
        shift = jnp.sum(jnp.sum(hits, axis=0, keepdims=True), axis=1, keepdims=True)
        across = jnp.broadcast_to(pno[pl.ds(p, 1), :], (rank, rank))
        diagonal = (across + across.T) - shift
        local_part[p] = 0.5 * ints[p].astype(jnp.float32) + diagonal * amps[p].astype(jnp.float32)

    @pl.loop(1, owners)
    def _(offset):
        edge_copy(offset).wait()

    def accumulate(j, total):
        total = total * late_scales[0, j] + recv_edge[within(late[0, j], edge_slots)].astype(jnp.float32)
        running[j] = total
        return total

    lax.fori_loop(0, edge_slots, accumulate, jnp.zeros((rank, rank), jnp.float32))

    @pl.loop(0, owners - 1)
    def _(step):
        offset = step_offset(step, owners)
        target = lax.rem(me + offset, owners)
        for k in range(mirror_cap):
            slot = target * mirror_cap + k
            p = within(late[2, slot], pairs)
            coupling = running[within(late[1, p], edge_slots)] * late_scales[1, p]
            send_half[slot] = (local_part[p] + coupling).astype(jnp.bfloat16)
        half_copy(offset).start()

    @pl.loop(0, owners - 1)
    def _(step):
        offset = step_offset(step, owners)
        half_copy(offset).wait_recv()
        sender = lax.rem(me - offset + owners, owners)
        for k in range(mirror_cap):
            slot = sender * mirror_cap + k
            flipped[slot] = recv_half[slot].astype(jnp.float32).T

    @pl.loop(0, pairs)
    def _(p):
        own_tile = send_half[within(late[4, p], half_slots)].astype(jnp.float32)
        out[p] = (own_tile + flipped[within(late[3, p], half_slots)]).astype(jnp.bfloat16)

    @pl.loop(1, owners)
    def _(offset):
        half_copy(offset).wait_send()


def local(
    amps, ints, pno_energy, occ_energy, pair_occ, mirror, edge_src, edge_dst, edge_fock, margin
):
    groups = lax.axis_size("grp")
    owners = lax.axis_size("own")
    pairs = amps.shape[0]
    rank = amps.shape[1]
    edge_count = edge_src.shape[0]
    occ_count = occ_energy.shape[0]
    mirror_cap = (pairs + owners - 2) // (owners - 1)
    edge_cap = (edge_count + owners - 2) // (owners - 1)
    edge_slots = owners * edge_cap
    half_slots = owners * mirror_cap
    occ_rows = -(-occ_count // LANES)
    widest = max(edge_count, edge_slots, half_slots, pairs, rank)
    width = -(-widest // LANES) * LANES

    height = -(-(2 * owners + 4 + occ_rows) // 8) * 8
    dims = (groups, owners, pairs, edge_cap, mirror_cap, occ_rows)
    vmem = pl.BlockSpec(memory_space=pltpu.VMEM)
    smem = pl.BlockSpec(memory_space=pltpu.SMEM)
    dma = pltpu.SemaphoreType.DMA
    return pl.pallas_call(
        functools.partial(kernel, dims),
        out_shape=jax.ShapeDtypeStruct(amps.shape, jnp.bfloat16),
        in_specs=[smem] + [vmem] * 9,
        out_specs=vmem,
        scratch_shapes=[
            pltpu.VMEM((edge_slots, rank, rank), jnp.bfloat16),
            pltpu.VMEM((edge_slots, rank, rank), jnp.bfloat16),
            pltpu.VMEM((edge_slots, rank, rank), jnp.float32),
            pltpu.VMEM((pairs, rank, rank), jnp.float32),
            pltpu.VMEM((half_slots, rank, rank), jnp.bfloat16),
            pltpu.VMEM((half_slots, rank, rank), jnp.bfloat16),
            pltpu.VMEM((half_slots, rank, rank), jnp.float32),
            pltpu.VMEM((groups, occ_rows, LANES), jnp.float32),
            pltpu.VMEM((owners, occ_rows, LANES), jnp.float32),
            pltpu.VMEM((height, width), jnp.float32),
            pltpu.VMEM((8, width), jnp.int32),
            pltpu.VMEM((8, width), jnp.float32),
            pltpu.VMEM((8, width), jnp.int32),
            pltpu.VMEM((8, width), jnp.float32),
            pltpu.SMEM((8, width), jnp.int32),
            pltpu.SMEM((8, width), jnp.float32),
            pltpu.SMEM((8, width), jnp.int32),
            pltpu.SMEM((8, width), jnp.float32),
            dma((4,)),
            dma((owners,)),
            dma((owners,)),
            dma((owners,)),
            dma((owners,)),
            dma((groups,)),
            dma((groups,)),
            dma((owners,)),
            dma((owners,)),
        ],
        compiler_params=pltpu.CompilerParams(
            collective_id=0, has_side_effects=True, vmem_limit_bytes=56 * 1024 * 1024
        ),
    )(
        pair_occ,
        occ_energy[None, :],
        mirror[None, :],
        edge_src[None, :],
        edge_dst[None, :],
        edge_fock[None, :],
        pno_energy,
        amps,
        ints,
        margin,
    )


def solution(mesh):
    in_specs = (
        P(("grp", "own"), None, None),
        P(("grp", "own"), None, None),
        P(("grp", "own"), None),
        P(),
        P(None, ("grp", "own")),
        P(("grp", "own")),
        P(("grp", "own")),
        P("grp"),
        P(("grp", "own")),
        P(("grp", "own"), None, None),
    )
    out_specs = P(("grp", "own"), None, None)
    return jax.shard_map(local, mesh=mesh, in_specs=in_specs, out_specs=out_specs, check_vma=False)
```
